32 devices in a mesh: gx: 8 (over z, core), gy: 4 (over y, x).
Axes of the slice: x: 2, y: 2, z: 4, core: 2. Of those that a mesh axis runs over, the one named last changes fastest.
Arguments:
- wave_tokens: bfloat16 [64, 128, 512], P('gx', 'gy'), may hold values from -6 to 6
- grad_out: bfloat16 [64, 128, 512], P('gx', 'gy'), may hold values from -6 to 6
- w_qkv: bfloat16 [512, 1536], replicated, may hold values from -0.25 to 0.25
- w_proj: bfloat16 [512, 512], replicated, may hold values from -0.25 to 0.25
- w_fc1: bfloat16 [512, 2048], replicated, may hold values from -0.25 to 0.25
- w_fc2: bfloat16 [2048, 512], replicated, may hold values from -0.125 to 0.125
- gain_attn: float32 [512], replicated, may hold values from 0.25 to 1.75
- gain_mlp: float32 [512], replicated, may hold values from 0.25 to 1.75
- attn_scale: float32 [16], replicated, may hold values from 2 to 16
- bias_table: float32 [16, 225], replicated, may hold values from -4 to 4
- r_wq: bfloat16 [512, 512], replicated, may hold values from -0.25 to 0.25
- r_wkv: bfloat16 [512, 1024], replicated, may hold values from -0.25 to 0.25
- r_wo: bfloat16 [512, 512], replicated, may hold values from -0.25 to 0.25
- read_scale: float32 [16], replicated, may hold values from 2 to 16
- floe_feat: bfloat16 [32, 768, 512], P(('gx', 'gy')), may hold values from -6 to 6
- floe_count: int32 [32], P(('gx', 'gy')), may hold values from 1 to 768, 8192 in all
- floe_patch: int32 [32, 768], P(('gx', 'gy')), may hold values from 0 to 8191, as said below
- floe_cover: int32 [32, 3, 768], P(('gx', 'gy')), may hold values 0 or 1
Outputs:
- patch_out: bfloat16 [64, 128, 512], P('gx', 'gy')
- grad_in: bfloat16 [64, 128, 512], P('gx', 'gy')
- floe_out: bfloat16 [32, 768, 512], P(('gx', 'gy'))
The draws below stay inside these ranges and needn't reach their ends.
Inputs may be any that keep to these rules, and one draw needn't show every extreme that they name: `floe_patch`: among one device's 768 slots, exactly 24 name a patch in each device's block of 8 x 32 patches. The live floes of a device are its first floe_count slots; the counts sum to 8192 and the largest is 768.
All inputs are finite; a program needn't handle non-finite values. No bound on the sum of `floe_cover` on one device may be relied on, other than what follows from the above.
Results may differ from the reference program's by a relative error of at most 0.02.
Values may be sent and summed in bfloat16 or wider, within the bound.
A program may use at most 128 MiB of HBM per device.

```python
import math
import jax
import jax.numpy as jnp
import numpy as np
from jax import lax

WIDTH = 512
HEADS = 16
FF = 2048
WIN = 8
SHIFT = 4
H_DEV = 8
W_DEV = 32
FLOE_MEAN = 256
NROWS = 64
NCOLS = 128
FLOE_CAP = 768
DEVICES = 32


def draw_floe_patch(key, part):
    dev_rows = NROWS // H_DEV
    dev_cols = NCOLS // W_DEV
    dev_total = dev_rows * dev_cols
    block_keys = jax.random.split(jax.random.fold_in(key, 11), dev_total)
    orders = jax.vmap(lambda block_key: jax.random.permutation(block_key, FLOE_CAP))(block_keys)
    target = orders % dev_total
    cell_pos = jax.random.randint(jax.random.fold_in(key, 12), (dev_total, FLOE_CAP), 0, H_DEV * W_DEV)
    row_pos = target // dev_cols * H_DEV + cell_pos // W_DEV
    col_pos = target % dev_cols * W_DEV + cell_pos % W_DEV
    return (row_pos * NCOLS + col_pos).astype(jnp.int32)


def set_ends(values, rng, low, high):
    extent = values.shape
    index_at = [jax.random.randint(jax.random.fold_in(rng, axis), (), 0, extent[axis]) for axis in range(len(extent))]
    values = values.at[tuple(index_at)].set(low)
    longest = extent.index(max(extent))
    index_at[longest] = (index_at[longest] + 1) % extent[longest]
    return values.at[tuple(index_at)].set(high)


def steps_of(key, shape, pieces, smallest, top_value):
    def one(axis_at, parts):
        steps = jax.random.uniform(jax.random.fold_in(jax.random.fold_in(key, 6), axis_at), (parts,), jnp.float32, smallest / len(pieces), top_value / len(pieces))
        return jnp.repeat(jnp.exp(steps), shape[axis_at] // parts).reshape((-1,) + (1,) * (len(shape) - axis_at - 1))

    gain = one(*pieces[0])
    for cut in pieces[1:]:
        gain = gain * one(*cut)
    return gain


def split_up(amount, total, most, skew):
    weights = [(1 << 20) // math.isqrt(grade ** skew) + 1 for grade in range(2, amount + 1)]
    surplus, counts = total - most - (amount - 1), [1] * (amount - 1)
    while surplus > 0:
        free = [i for i in range(amount - 1) if counts[i] < most]
        whole, budget = sum([weights[i] for i in free]), surplus
        for i in free:
            more = min(most - counts[i], max(1, budget * weights[i] // whole), surplus)
            counts[i] = counts[i] + more
            surplus = surplus - more
    return np.array([most] + counts)


def uneven(rng, number_of, total, most, skew):
    if number_of == 2:
        one = jax.random.randint(rng, (), max(1, total - most), min(most, total - 1) + 1)
        return jnp.stack([one, total - one])
    tallies = jnp.asarray(split_up(number_of, total, most, skew), jnp.int32)
    pairs = (number_of - 1) // 2
    giver, taker = tallies[1:1 + 2 * pairs:2], tallies[2:2 + 2 * pairs:2]
    slack = jnp.minimum(giver - 1, most - taker)
    passed = jax.random.randint(jax.random.fold_in(rng, 1), (pairs,), 0, 1 << 20) % (slack + 1)
    tallies = tallies.at[1:1 + 2 * pairs:2].set(giver - passed).at[2:2 + 2 * pairs:2].set(taker + passed)
    return tallies[jax.random.permutation(jax.random.fold_in(rng, 2), number_of)]


def noise(own_key, shape, deviation, bound, cuts=(), held_as=jnp.bfloat16):
    entries = jax.random.normal(own_key, shape, jnp.float32) * deviation
    if len(cuts) > 0:
        entries = steps_of(own_key, shape, cuts, -0.22, 0.18) * entries
    return jnp.clip(entries, min=-bound, max=bound).astype(held_as)


def setup_inputs(seed: int = 0) -> dict:
    seeds = jax.random.split(jax.random.key(seed), 19)
    wave_tokens = noise(seeds[0], (NROWS, NCOLS, WIDTH), 1.0, 6.0, ((0, 8), (1, 4)))
    grad_out = noise(seeds[1], (NROWS, NCOLS, WIDTH), 1.0, 6.0, ((0, 8), (1, 4)))
    w_qkv = noise(seeds[2], (WIDTH, 3 * WIDTH), WIDTH ** -0.5, 0.25)
    w_proj = noise(seeds[3], (WIDTH, WIDTH), WIDTH ** -0.5, 0.25)
    w_fc1 = noise(seeds[4], (WIDTH, FF), WIDTH ** -0.5, 0.25)
    w_fc2 = noise(seeds[5], (FF, WIDTH), FF ** -0.5, 0.125)
    gain_attn = jnp.clip(1.0 + 0.15 * jax.random.normal(seeds[6], (WIDTH,), jnp.float32), 0.25, 1.75)
    gain_mlp = jnp.clip(1.0 + 0.15 * jax.random.normal(seeds[7], (WIDTH,), jnp.float32), 0.25, 1.75)
    attn_scale = jnp.clip(jnp.exp(jax.random.uniform(seeds[8], (HEADS,), jnp.float32, math.log(2.0), math.log(16.0))), 2.0, 16.0)
    bias_table = noise(seeds[9], (HEADS, (2 * WIN - 1) * (2 * WIN - 1)), 1.0, 4.0, (), jnp.float32)
    r_wq = noise(seeds[10], (WIDTH, WIDTH), WIDTH ** -0.5, 0.25)
    r_wkv = noise(seeds[11], (WIDTH, 2 * WIDTH), WIDTH ** -0.5, 0.25)
    r_wo = noise(seeds[12], (WIDTH, WIDTH), WIDTH ** -0.5, 0.25)
    read_scale = jnp.clip(jnp.exp(jax.random.uniform(seeds[13], (HEADS,), jnp.float32, math.log(2.0), math.log(16.0))), 2.0, 16.0)
    floe_feat = noise(seeds[14], (DEVICES, FLOE_CAP, WIDTH), 1.0, 6.0, ((0, 32),))
    floe_count = uneven(seeds[15], DEVICES, DEVICES * FLOE_MEAN, FLOE_CAP, 2).astype(jnp.int32)
    floe_patch = draw_floe_patch(jax.random.fold_in(seeds[18], 71), 0)
    floe_cover = set_ends((jax.random.randint(seeds[17], (DEVICES, 3, FLOE_CAP), 0, 2) < 1).astype(jnp.int32), jax.random.fold_in(seeds[17], 1), 0, 1)
    return dict(wave_tokens=wave_tokens, grad_out=grad_out, w_qkv=w_qkv, w_proj=w_proj, w_fc1=w_fc1, w_fc2=w_fc2, gain_attn=gain_attn, gain_mlp=gain_mlp, attn_scale=attn_scale, bias_table=bias_table, r_wq=r_wq, r_wkv=r_wkv, r_wo=r_wo, read_scale=read_scale, floe_feat=floe_feat, floe_count=floe_count, floe_patch=floe_patch, floe_cover=floe_cover)


def layer_norm(values):
    centred = values - lax.optimization_barrier(jnp.mean(values, -1, keepdims=True))
    return centred / jnp.sqrt(lax.optimization_barrier(jnp.mean(centred * centred, -1, keepdims=True)) + 1e-05)

def unit_heads(values):
    return values / jnp.maximum(jnp.sqrt(lax.optimization_barrier(jnp.sum(values * values, -1, keepdims=True))), 1.0)

def bias_index(window):
    grid_pos = np.stack(np.meshgrid(np.arange(window), np.arange(window), indexing='ij')).reshape(2, -1)
    offsets = grid_pos[:, :, None] - grid_pos[:, None, :] + window - 1
    return offsets[0] * (2 * window - 1) + offsets[1]

def swin_block(field, w_qkv, w_proj, w_fc1, w_fc2, gain_attn, gain_mlp, attn_scale, bias_full):
    tok_rows, tok_cols, feat_width = field.shape
    head_count = attn_scale.shape[0]
    head_size = feat_width // head_count
    span = WIN * WIN
    windows = field.reshape(tok_rows // WIN, WIN, tok_cols // WIN, WIN, feat_width).transpose(0, 2, 1, 3, 4).reshape(-1, feat_width)
    win_count = windows.shape[0] // span
    qkv_all = jnp.dot(windows, w_qkv, preferred_element_type=jnp.float32).astype(jnp.bfloat16)
    qkv_all = lax.optimization_barrier(qkv_all)
    qkv_all = qkv_all.reshape(win_count, span, 3, head_count, head_size)
    queries = unit_heads(qkv_all[:, :, 0].astype(jnp.float32))
    keys_unit = unit_heads(qkv_all[:, :, 1].astype(jnp.float32))
    scores = jnp.einsum('wihd,wjhd->whij', queries, keys_unit, precision=lax.Precision.HIGHEST)
    scores = scores * attn_scale[None, :, None, None] + bias_full[None]
    expo = jnp.exp(scores)
    probs = (expo / lax.optimization_barrier(jnp.sum(expo, -1, keepdims=True))).astype(jnp.bfloat16)
    mixed = jnp.einsum('whij,wjhd->wihd', probs, qkv_all[:, :, 2], preferred_element_type=jnp.float32)
    mixed = mixed.astype(jnp.bfloat16).reshape(-1, feat_width)
    attn_out = jnp.dot(mixed, w_proj, preferred_element_type=jnp.float32)
    hidden_one = (windows.astype(jnp.float32) + layer_norm(attn_out) * gain_attn).astype(jnp.bfloat16)
    hidden_one = lax.optimization_barrier(hidden_one)
    inner = jax.nn.gelu(jnp.dot(hidden_one, w_fc1, preferred_element_type=jnp.float32), approximate=True).astype(jnp.bfloat16)
    mlp_out = jnp.dot(inner, w_fc2, preferred_element_type=jnp.float32)
    result = (hidden_one.astype(jnp.float32) + layer_norm(mlp_out) * gain_mlp).astype(jnp.bfloat16)
    result = result.reshape(tok_rows // WIN, tok_cols // WIN, WIN, WIN, feat_width).transpose(0, 2, 1, 3, 4)
    return result.reshape(tok_rows, tok_cols, feat_width)

def readout_mix(query, key_vals, flags, read_scale):
    floe_rows, feat_width = query.shape
    head_count = read_scale.shape[0]
    head_size = feat_width // head_count
    query_unit = unit_heads(query.astype(jnp.float32).reshape(floe_rows, head_count, head_size))
    key_unit = unit_heads(key_vals[:, :, :feat_width].astype(jnp.float32).reshape(floe_rows, 4, head_count, head_size))
    values = key_vals[:, :, feat_width:].astype(jnp.float32).reshape(floe_rows, 4, head_count, head_size)
    scores = lax.optimization_barrier(jnp.sum(query_unit[:, None] * key_unit, -1)) * read_scale
    expo = jnp.exp(scores) * flags[:, :, None]
    weights = expo / lax.optimization_barrier(jnp.sum(expo, 1, keepdims=True))
    return lax.optimization_barrier(jnp.sum(weights[..., None] * values, 1)).reshape(floe_rows, feat_width).astype(jnp.bfloat16)

def reference(wave_tokens, grad_out, w_qkv, w_proj, w_fc1, w_fc2, gain_attn, gain_mlp, attn_scale, bias_table, r_wq, r_wkv, r_wo, read_scale, floe_feat, floe_count, floe_patch, floe_cover):
    bias_full = bias_table[:, bias_index(WIN)]

    def local_block(field):
        return swin_block(field, w_qkv, w_proj, w_fc1, w_fc2, gain_attn, gain_mlp, attn_scale, bias_full)
    rolled = jnp.roll(wave_tokens, (-SHIFT, -SHIFT), (0, 1))
    cot_rolled = jnp.roll(grad_out, (-SHIFT, -SHIFT), (0, 1))

    def band_step(pair):
        band_in, band_cot = pair
        band_out, pull_back = jax.vjp(local_block, band_in)
        return (band_out, pull_back(band_cot)[0])
    band_out, band_grad = lax.map(band_step, (rolled.reshape(NROWS // WIN, WIN, NCOLS, WIDTH), cot_rolled.reshape(NROWS // WIN, WIN, NCOLS, WIDTH)))
    patch_out = jnp.roll(band_out.reshape(NROWS, NCOLS, WIDTH), (SHIFT, SHIFT), (0, 1))
    grad_in = jnp.roll(band_grad.reshape(NROWS, NCOLS, WIDTH), (SHIFT, SHIFT), (0, 1))
    key_all = jnp.dot(patch_out.reshape(-1, WIDTH), r_wkv, preferred_element_type=jnp.float32).astype(jnp.bfloat16)

    def floe_block(item):
        feat, live, patch, cover = item
        row_pos = patch // NCOLS
        col_pos = patch % NCOLS
        row_next = (row_pos + 1) % NROWS
        col_next = (col_pos + 1) % NCOLS
        index_set = jnp.stack([row_pos * NCOLS + col_pos, row_pos * NCOLS + col_next, row_next * NCOLS + col_pos, row_next * NCOLS + col_next], -1).astype(jnp.int32)
        key_vals = key_all[index_set]
        flags = jnp.stack([jnp.ones_like(cover[0]), cover[0], cover[1], cover[2]], -1).astype(jnp.float32)
        query = jnp.dot(feat, r_wq, preferred_element_type=jnp.float32).astype(jnp.bfloat16)
        floe_mix = readout_mix(query, key_vals, flags, read_scale)
        updated = feat.astype(jnp.float32) + jnp.dot(floe_mix, r_wo, preferred_element_type=jnp.float32)
        alive = jnp.arange(FLOE_CAP, dtype=jnp.int32) < live
        return jnp.where(alive[:, None], updated, 0.0).astype(jnp.bfloat16)
    floe_out = lax.map(floe_block, (floe_feat, floe_count, floe_patch, floe_cover))
    return (patch_out, grad_in, floe_out)
```

```python
import jax
import jax.numpy as jnp
import numpy as np
from jax import lax
from jax.experimental import pallas as pl
from jax.experimental.pallas import tpu as pltpu
from jax.sharding import PartitionSpec as P

WIN = 8
SHIFT = 4
SPAN = WIN * WIN
LANES = 128
F32 = jnp.float32
BF16 = jnp.bfloat16
GELU_A = 0.7978845608028654
GELU_B = 0.044715
NN = (((1,), (0,)), ((), ()))
NT = (((1,), (1,)), ((), ()))
TN = (((0,), (0,)), ((), ()))


def dot(a, b, dims=NN):
    return lax.dot_general(a, b, dims, preferred_element_type=F32)


def split_dot(values, ones):
    high = values.astype(BF16)
    low = (values - high.astype(F32)).astype(BF16)
    return dot(jnp.concatenate([high, low], 1), ones)


def block_ones(rows, cols, row_size, col_size):
    r = lax.broadcasted_iota(jnp.int32, (rows, cols), 0) // row_size
    c = lax.broadcasted_iota(jnp.int32, (rows, cols), 1) // col_size
    return jnp.where(r == c, 1.0, 0.0).astype(BF16)


def to_windows(block):
    rows, cols, width = block.shape
    parts = [block[:, w * WIN : (w + 1) * WIN, :].reshape(SPAN, width) for w in range(cols // WIN)]
    return jnp.concatenate(parts, 0)


def from_windows(flat):
    count = flat.shape[0] // SPAN
    parts = [flat[w * SPAN : (w + 1) * SPAN].reshape(WIN, WIN, flat.shape[1]) for w in range(count)]
    return jnp.concatenate(parts, 1)


def norm_parts(values):
    mean = jnp.mean(values, -1, keepdims=True)
    centred = values - mean
    inv = lax.rsqrt(jnp.mean(centred * centred, -1, keepdims=True) + 1e-05)
    return centred * inv, inv


def norm_back(cot, unit, inv):
    return inv * (
        cot - jnp.mean(cot, -1, keepdims=True) - unit * jnp.mean(cot * unit, -1, keepdims=True)
    )


def forward_kernel(
    x_ref, w_qkv, w_proj, w_fc1, w_fc2, gain_attn, gain_mlp, scale_ref, bias_ref,
    out_ref, qs_ref, kn_ref, v_ref, rq_ref, rk_ref, p_ref, mixed_ref, u1_ref, i1_ref, dg_ref, u2_ref, i2_ref,
):
    width = x_ref.shape[-1]
    head = width // (bias_ref.shape[1] // SPAN)
    per = LANES // head
    x = to_windows(x_ref[...].astype(F32))
    xb = x.astype(BF16)
    windows = x.shape[0] // SPAN
    sum_ones = block_ones(LANES, LANES, head, head)
    sum_ones = jnp.concatenate([sum_ones, sum_ones], 0)
    mask = block_ones(per * SPAN, LANES, SPAN, head)
    key_ones = block_ones(per * SPAN, per * SPAN, SPAN, SPAN)
    for g in range(width // LANES):
        at = slice(g * LANES, (g + 1) * LANES)
        q = dot(xb, w_qkv[:, at]).astype(BF16).astype(F32)
        k = dot(xb, w_qkv[:, width + g * LANES : width + (g + 1) * LANES]).astype(BF16).astype(F32)
        v = dot(xb, w_qkv[:, 2 * width + g * LANES : 2 * width + (g + 1) * LANES]).astype(BF16)
        q2 = split_dot(q * q, sum_ones)
        k2 = split_dot(k * k, sum_ones)
        rq = jnp.where(q2 > 1.0, lax.rsqrt(q2), 1.0)
        rk = jnp.where(k2 > 1.0, lax.rsqrt(k2), 1.0)
        rq_ref[:, at] = jnp.where(q2 == 1.0, -1.0, rq)
        rk_ref[:, at] = jnp.where(k2 == 1.0, -1.0, rk)
        qs = (q * rq * scale_ref[:, at]).astype(BF16)
        kn = (k * rk).astype(BF16)
        qs_ref[:, at] = qs
        kn_ref[:, at] = kn
        v_ref[:, at] = v
        bias = bias_ref[:, g * per * SPAN : (g + 1) * per * SPAN]
        for w in range(windows):
            rows = slice(w * SPAN, (w + 1) * SPAN)
            kb = jnp.concatenate([kn[rows]] * per, 0) * mask
            vb = jnp.concatenate([v[rows]] * per, 0) * mask
            expo = jnp.exp(dot(qs[rows], kb, NT) + bias)
            total = dot(expo.astype(BF16), key_ones)
            p = (expo / total).astype(BF16)
            p_ref[(g * windows + w) * SPAN : (g * windows + w + 1) * SPAN, :] = p
            mixed_ref[rows, at] = dot(p, vb).astype(BF16)
    u1, i1 = norm_parts(dot(mixed_ref[...], w_proj[...]))
    u1_ref[...] = u1
    i1_ref[...] = i1
    h1 = (x + u1 * gain_attn[...]).astype(BF16)
    mlp = jnp.zeros(x.shape, F32)
    step = width
    for c in range(w_fc1.shape[1] // step):
        cols = slice(c * step, (c + 1) * step)
        z = dot(h1, w_fc1[:, cols])
        zz = z * z
        t = jnp.tanh(GELU_A * z * (1.0 + GELU_B * zz))
        half = 0.5 * (1.0 + t)
        dg_ref[:, cols] = half + 0.5 * z * (1.0 - t * t) * (GELU_A + 3.0 * GELU_A * GELU_B * zz)
        mlp = mlp + dot((z * half).astype(BF16), w_fc2[cols, :])
    u2, i2 = norm_parts(mlp)
    u2_ref[...] = u2
    i2_ref[...] = i2
    out_ref[...] = from_windows(h1.astype(F32) + u2 * gain_mlp[...]).astype(BF16)


def unit_back(cot, unit, inv, sum_ones):
    along = split_dot(cot * unit, sum_ones)
    part = jnp.where(inv < 0.0, 0.5, jnp.where(inv < 1.0, 1.0, 0.0))
    return jnp.abs(inv) * (cot - part * unit * along)


def backward_kernel(
    cot_ref, w_qkv, w_proj, w_fc1, w_fc2, gain_attn, gain_mlp, scale_ref,
    qs_ref, kn_ref, v_ref, rq_ref, rk_ref, p_ref, mixed_ref, u1_ref, i1_ref, dg_ref, u2_ref, i2_ref,
    grad_ref, dm_ref,
):
    width = cot_ref.shape[-1]
    per = p_ref.shape[1] // SPAN
    head = LANES // per
    cot = to_windows(cot_ref[...].astype(F32))
    windows = cot.shape[0] // SPAN
    dmlp = norm_back(cot * gain_mlp[...], u2_ref[...], i2_ref[...]).astype(BF16)
    dh = jnp.zeros(cot.shape, F32)
    step = width
    for c in range(w_fc1.shape[1] // step):
        cols = slice(c * step, (c + 1) * step)
        dz = dot(dmlp, w_fc2[cols, :], NT) * dg_ref[:, cols]
        dh = dh + dot(dz.astype(BF16), w_fc1[:, cols], NT)
    dh = (cot + dh).astype(BF16).astype(F32)
    dproj = norm_back(dh * gain_attn[...], u1_ref[...], i1_ref[...]).astype(BF16)
    dm_ref[...] = dot(dproj, w_proj[...], NT).astype(BF16)
    sum_ones = block_ones(LANES, LANES, head, head)
    sum_ones = jnp.concatenate([sum_ones, sum_ones], 0)
    mask = block_ones(per * SPAN, LANES, SPAN, head)
    mask32 = mask.astype(F32)
    dx = dh
    for g in range(width // LANES):
        at = slice(g * LANES, (g + 1) * LANES)
        dm = dm_ref[:, at]
        own = (dm.astype(F32) * mixed_ref[:, at].astype(F32)).astype(BF16)
        both = jnp.concatenate([dm, own], 1)
        qs = qs_ref[:, at]
        kn = kn_ref[:, at]
        v = v_ref[:, at]
        dqs, dks, dvs = [], [], []
        for w in range(windows):
            rows = slice(w * SPAN, (w + 1) * SPAN)
            kb = jnp.concatenate([kn[rows]] * per, 0) * mask
            vb = jnp.concatenate([v[rows]] * per, 0) * mask
            p = p_ref[(g * windows + w) * SPAN : (g * windows + w + 1) * SPAN, :]
            spread = dot(both[rows], jnp.concatenate([vb, -mask], 1), NT)
            ds = (p.astype(F32) * spread).astype(BF16)
            dqs.append(dot(ds, kb))
            dkb = dot(ds, qs[rows], TN) * mask32
            dvb = dot(p, dm[rows], TN) * mask32
            dks.append(sum(dkb[i * SPAN : (i + 1) * SPAN] for i in range(per)))
            dvs.append(sum(dvb[i * SPAN : (i + 1) * SPAN] for i in range(per)))
        scale = scale_ref[:, at]
        dq = unit_back(
            jnp.concatenate(dqs, 0) * scale, qs.astype(F32) / scale, rq_ref[:, at], sum_ones
        )
        dk = unit_back(jnp.concatenate(dks, 0), kn.astype(F32), rk_ref[:, at], sum_ones)
        dv = jnp.concatenate(dvs, 0)
        dx = dx + dot(dq.astype(BF16), w_qkv[:, at], NT)
        dx = dx + dot(dk.astype(BF16), w_qkv[:, width + g * LANES : width + (g + 1) * LANES], NT)
        dx = dx + dot(dv.astype(BF16), w_qkv[:, 2 * width + g * LANES : 2 * width + (g + 1) * LANES], NT)
    grad_ref[...] = from_windows(dx).astype(BF16)


def order_kernel(tok_rows, tok_cols, row_devs, col_devs, feat_ref, patch_ref, cover_ref, w_ref, send_ref, pos_ref):
    slots, width = feat_ref.shape
    devs = row_devs * col_devs
    grid_cols = tok_cols * col_devs
    patch = patch_ref[...]
    row = patch // grid_cols
    col = patch % grid_cols
    target = row // tok_rows * col_devs + col // tok_cols
    hit = lax.broadcasted_iota(jnp.int32, (devs, slots), 0) == target
    i = lax.broadcasted_iota(jnp.int32, (slots, slots), 0)
    j = lax.broadcasted_iota(jnp.int32, (slots, slots), 1)
    earlier = jnp.where(i < j, 1.0, 0.0).astype(BF16)
    count = dot(jnp.where(hit, 1.0, 0.0).astype(BF16), earlier)
    rank = jnp.sum(jnp.where(hit, count, 0.0), 0, keepdims=True).astype(jnp.int32)
    pos = target * (slots // devs) + rank
    pos_ref[...] = pos
    place = jnp.where(i == pos, 1.0, 0.0).astype(BF16)
    query = dot(feat_ref[...], w_ref[...]).astype(BF16)
    send_ref[:, :width] = dot(place, query).astype(BF16)
    which = lax.broadcasted_iota(jnp.int32, (LANES, slots), 0)
    meta = jnp.where(which == 0, (row % tok_rows).astype(F32), 0.0)
    meta = jnp.where(which == 1, (col % tok_cols).astype(F32), meta)
    for c in range(3):
        meta = jnp.where(which == 2 + c, cover_ref[c : c + 1, :].astype(F32), meta)
    send_ref[:, width:] = dot(place, meta.astype(BF16), NT).astype(BF16)


def readout_kernel(cols, piece_ref, ext_ref, w_ref, scale_ref, head, out_ref, table_ref):
    width = out_ref.shape[1]
    rows = out_ref.shape[0]
    cells = ext_ref.shape[0]
    sum_ones = block_ones(LANES, LANES, head, head)
    sum_ones = jnp.concatenate([sum_ones, sum_ones], 0)

    @pl.when(pl.program_id(0) == 0)
    def _():
        for g in range(width // LANES):
            at = slice(g * LANES, (g + 1) * LANES)
            k = dot(ext_ref[...], w_ref[:, at]).astype(BF16).astype(F32)
            k2 = split_dot(k * k, sum_ones)
            table_ref[:, at] = (k * jnp.where(k2 > 1.0, lax.rsqrt(k2), 1.0)).astype(BF16)
        table_ref[:, width:] = dot(ext_ref[...], w_ref[:, width:]).astype(BF16)

    meta = piece_ref[:, width : width + LANES].astype(F32)
    base = (meta[:, 0:1] * cols + meta[:, 1:2]).astype(jnp.int32)
    lane = lax.broadcasted_iota(jnp.int32, (rows, cells), 1)
    picks = [
        jnp.where(lane == base + step, 1.0, 0.0).astype(BF16) for step in (0, 1, cols, cols + 1)
    ]
    flags = [None] + [meta[:, 2 + c : 3 + c] for c in range(3)]
    for g in range(width // LANES):
        at = slice(g * LANES, (g + 1) * LANES)
        q = piece_ref[:, at].astype(F32)
        q2 = split_dot(q * q, sum_ones)
        q = q * jnp.where(q2 > 1.0, lax.rsqrt(q2), 1.0) * scale_ref[:, at]
        both = jnp.concatenate([table_ref[:, at], table_ref[:, width + g * LANES : width + (g + 1) * LANES]], 1)
        total, mix = 0.0, 0.0
        for pick, flag in zip(picks, flags):
            got = dot(pick, both)
            expo = jnp.exp(split_dot(q * got[:, :LANES], sum_ones))
            if flag is not None:
                expo = expo * flag
            total = total + expo
            mix = mix + expo * got[:, LANES:]
        out_ref[:, at] = (mix / total).astype(BF16)


def finish_kernel(ret_ref, pos_ref, feat_ref, w_ref, live_ref, out_ref):
    slots = feat_ref.shape[0]
    i = lax.broadcasted_iota(jnp.int32, (slots, slots), 0)
    place = jnp.where(i == pos_ref[...], 1.0, 0.0).astype(BF16)
    mix = dot(place, ret_ref[...], TN).astype(BF16)
    updated = feat_ref[...].astype(F32) + dot(mix, w_ref[...])
    slot = lax.broadcasted_iota(jnp.int32, updated.shape, 0)
    out_ref[...] = jnp.where(slot < live_ref[0], updated, 0.0).astype(BF16)


def bias_index():
    grid_pos = np.stack(np.meshgrid(np.arange(WIN), np.arange(WIN), indexing="ij")).reshape(2, -1)
    offsets = grid_pos[:, :, None] - grid_pos[:, None, :] + WIN - 1
    return offsets[0] * (2 * WIN - 1) + offsets[1]


def moved(piece, rows, cols):
    n, m = lax.axis_size("gx"), lax.axis_size("gy")
    route = [
        (i * m + j, (i + rows) % n * m + (j + cols) % m) for i in range(n) for j in range(m)
    ]
    return lax.ppermute(piece, ("gx", "gy"), route)


def params(mib=48):
    return pltpu.CompilerParams(vmem_limit_bytes=mib * 1024 * 1024)


def local(
    wave_tokens, grad_out, w_qkv, w_proj, w_fc1, w_fc2, gain_attn, gain_mlp, attn_scale,
    bias_table, r_wq, r_wkv, r_wo, read_scale, floe_feat, floe_count, floe_patch, floe_cover,
):
    tok_rows, tok_cols, width = wave_tokens.shape
    heads = attn_scale.shape[0]
    head = width // heads
    tokens = tok_rows * tok_cols
    hidden = w_fc1.shape[1]
    row_devs, col_devs = lax.axis_size("gx"), lax.axis_size("gy")
    feat = floe_feat[0]
    slots = feat.shape[0]
    vmem = pl.BlockSpec(memory_space=pltpu.VMEM)
    s = SHIFT

    row_in = moved(jnp.concatenate([wave_tokens[:s, s:], grad_out[:s, s:]], 0), -1, 0)
    col_in = moved(jnp.concatenate([wave_tokens[s:, :s], grad_out[s:, :s]], 0), 0, -1)
    cor_in = moved(jnp.concatenate([wave_tokens[:s, :s], grad_out[:s, :s]], 0), -1, -1)

    def ahead(field, part):
        upper = jnp.concatenate([field[s:, s:], col_in[part * (tok_rows - s) : (part + 1) * (tok_rows - s)]], 1)
        lower = jnp.concatenate([row_in[part * s : (part + 1) * s], cor_in[part * s : (part + 1) * s]], 1)
        return jnp.concatenate([upper, lower], 0)

    send, pos = pl.pallas_call(
        lambda *refs: order_kernel(tok_rows, tok_cols, row_devs, col_devs, *refs),
        out_shape=(
            jax.ShapeDtypeStruct((slots, width + LANES), BF16),
            jax.ShapeDtypeStruct((1, slots), jnp.int32),
        ),
        in_specs=[vmem] * 4,
        out_specs=(vmem, vmem),
        compiler_params=params(),
        cost_estimate=pl.CostEstimate(flops=3000000000, bytes_accessed=3000000, transcendentals=0),
    )(feat, floe_patch, floe_cover[0], r_wq)
    piece = lax.all_to_all(send, ("gx", "gy"), split_axis=0, concat_axis=0, tiled=True)

    bias = bias_table[:, bias_index()].transpose(1, 0, 2).reshape(SPAN, heads * SPAN)
    scale = jnp.repeat(attn_scale, head)[None]
    gain_a, gain_m = gain_attn[None], gain_mlp[None]
    rolled = ahead(wave_tokens, 0)
    cot = ahead(grad_out, 1)
    wide = jax.ShapeDtypeStruct((tokens, width), BF16)
    wide32 = jax.ShapeDtypeStruct((tokens, width), F32)
    one = jax.ShapeDtypeStruct((tokens, 1), F32)
    res = pl.pallas_call(
        forward_kernel,
        out_shape=(
            jax.ShapeDtypeStruct(wave_tokens.shape, BF16),
            wide, wide, wide, wide32, wide32,
            jax.ShapeDtypeStruct((tokens * width // LANES, LANES // head * SPAN), BF16),
            wide, wide32, one, jax.ShapeDtypeStruct((tokens, hidden), F32), wide32, one,
        ),
        in_specs=[vmem] * 9,
        out_specs=(vmem,) * 13,
        compiler_params=params(),
        cost_estimate=pl.CostEstimate(flops=8000000000, bytes_accessed=8000000, transcendentals=1000000),
    )(rolled, w_qkv, w_proj, w_fc1, w_fc2, gain_a, gain_m, scale, bias)
    out = res[0]
    near, far = tok_rows - s + 1, tok_cols - s
    row_out = moved(out[s:, : far + 1], 1, 0)
    col_out = moved(out[:near, far:], 0, 1)
    cor_out = moved(out[s:, far:], 1, 1)
    grad = pl.pallas_call(
        backward_kernel,
        out_shape=jax.ShapeDtypeStruct(wave_tokens.shape, BF16),
        in_specs=[vmem] * 20,
        out_specs=vmem,
        scratch_shapes=[pltpu.VMEM((tokens, width), BF16)],
        compiler_params=params(),
        cost_estimate=pl.CostEstimate(flops=10000000000, bytes_accessed=8000000, transcendentals=0),
    )(cot, w_qkv, w_proj, w_fc1, w_fc2, gain_a, gain_m, scale, *res[1:])
    row_grad = moved(grad[s:, :far], 1, 0)
    col_grad = moved(grad[: tok_rows - s, far:], 0, 1)
    cor_grad = moved(grad[s:, far:], 1, 1)

    ext = jnp.concatenate(
        [
            jnp.concatenate([cor_out, row_out], 1),
            jnp.concatenate([col_out, out[:near, : far + 1]], 1),
        ],
        0,
    )
    patch_out = ext[:tok_rows, :tok_cols]
    ext_cols = tok_cols + 1
    cells = (tok_rows + 1) * ext_cols
    padded = -(-cells // LANES) * LANES
    table = jnp.pad(ext.reshape(cells, width), ((0, padded - cells), (0, 0)))
    parts = 3
    chunk = slots // parts
    mix = pl.pallas_call(
        lambda a, b, c, d, e, f: readout_kernel(ext_cols, a, b, c, d, head, e, f),
        out_shape=jax.ShapeDtypeStruct((slots, width), BF16),
        grid=(parts,),
        in_specs=[
            pl.BlockSpec((chunk, width + LANES), lambda i: (i, 0)),
            vmem, vmem, vmem,
        ],
        out_specs=pl.BlockSpec((chunk, width), lambda i: (i, 0)),
        scratch_shapes=[pltpu.VMEM((padded, 2 * width), BF16)],
        compiler_params=params(),
        cost_estimate=pl.CostEstimate(flops=8000000000, bytes_accessed=3000000, transcendentals=1000000),
    )(piece, table, r_wkv, jnp.repeat(read_scale, head)[None])
    back = lax.all_to_all(mix, ("gx", "gy"), split_axis=0, concat_axis=0, tiled=True)
    floe_out = pl.pallas_call(
        finish_kernel,
        out_shape=jax.ShapeDtypeStruct((slots, width), BF16),
        in_specs=[vmem] * 4 + [pl.BlockSpec(memory_space=pltpu.SMEM)],
        out_specs=vmem,
        compiler_params=params(),
        cost_estimate=pl.CostEstimate(flops=1500000000, bytes_accessed=3000000, transcendentals=0),
    )(back, pos, feat, r_wo, floe_count)
    grad_in = jnp.concatenate(
        [
            jnp.concatenate([cor_grad, row_grad], 1),
            jnp.concatenate([col_grad, grad[: tok_rows - s, :far]], 1),
        ],
        0,
    )
    return (patch_out, grad_in, floe_out[None])


def solution(mesh):
    grid = P("gx", "gy", None)
    owner = ("gx", "gy")
    in_specs = (grid, grid) + (P(),) * 12 + (P(owner, None, None), P(owner), P(owner, None), P(owner, None, None))
    out_specs = (grid, grid, P(owner, None, None))
    return jax.shard_map(local, mesh=mesh, in_specs=in_specs, out_specs=out_specs, check_vma=False)
```

```python
import jax
import jax.numpy as jnp
from jax import lax
from jax.experimental import pallas as pl
from jax.experimental.pallas import tpu as pltpu
from jax.sharding import PartitionSpec as P

WIN = 8
SHIFT = 4
SPAN = WIN * WIN
LANES = 128
F32 = jnp.float32
BF16 = jnp.bfloat16
GELU_A = 0.7978845608028654
GELU_B = 0.044715
NN = (((1,), (0,)), ((), ()))
NT = (((1,), (1,)), ((), ()))
TN = (((0,), (0,)), ((), ()))


def dot(a, b, dims=NN):
    return lax.dot_general(a, b, dims, preferred_element_type=F32)


def split_dot(values, ones):
    high = values.astype(BF16)
    low = (values - high.astype(F32)).astype(BF16)
    return dot(jnp.concatenate([high, low], 1), ones)


def block_ones(rows, cols, row_size, col_size):
    r = lax.broadcasted_iota(jnp.int32, (rows, cols), 0) // row_size
    c = lax.broadcasted_iota(jnp.int32, (rows, cols), 1) // col_size
    return jnp.where(r == c, 1.0, 0.0).astype(BF16)


def to_windows(block):
    rows, cols, width = block.shape
    parts = [block[:, w * WIN : (w + 1) * WIN, :].reshape(SPAN, width) for w in range(cols // WIN)]
    return jnp.concatenate(parts, 0)


def from_windows(flat):
    count = flat.shape[0] // SPAN
    parts = [flat[w * SPAN : (w + 1) * SPAN].reshape(WIN, WIN, flat.shape[1]) for w in range(count)]
    return jnp.concatenate(parts, 1)


def norm_parts(values):
    mean = jnp.mean(values, -1, keepdims=True)
    centred = values - mean
    inv = lax.rsqrt(jnp.mean(centred * centred, -1, keepdims=True) + 1e-05)
    return centred * inv, inv


def norm_back(cot, unit, inv):
    return inv * (
        cot - jnp.mean(cot, -1, keepdims=True) - unit * jnp.mean(cot * unit, -1, keepdims=True)
    )


def forward_kernel(
    x_ref, w_qkv, w_proj, w_fc1, w_fc2, gain_attn, gain_mlp, scale_ref, bias_ref,
    out_ref, qs_ref, kn_ref, v_ref, rq_ref, rk_ref, p_ref, mixed_ref, u1_ref, i1_ref, dg_ref, u2_ref, i2_ref,
):
    width = x_ref.shape[-1]
    head = width // (bias_ref.shape[1] // SPAN)
    per = LANES // head
    x = to_windows(x_ref[...].astype(F32))
    xb = x.astype(BF16)
    windows = x.shape[0] // SPAN
    sum_ones = block_ones(LANES, LANES, head, head)
    sum_ones = jnp.concatenate([sum_ones, sum_ones], 0)
    mask = block_ones(per * SPAN, LANES, SPAN, head)
    key_ones = block_ones(per * SPAN, per * SPAN, SPAN, SPAN)
    for g in range(width // LANES):
        at = slice(g * LANES, (g + 1) * LANES)
        q = dot(xb, w_qkv[:, at]).astype(BF16).astype(F32)
        k = dot(xb, w_qkv[:, width + g * LANES : width + (g + 1) * LANES]).astype(BF16).astype(F32)
        v = dot(xb, w_qkv[:, 2 * width + g * LANES : 2 * width + (g + 1) * LANES]).astype(BF16)
        q2 = split_dot(q * q, sum_ones)
        k2 = split_dot(k * k, sum_ones)
        rq = jnp.where(q2 > 1.0, lax.rsqrt(q2), 1.0)
        rk = jnp.where(k2 > 1.0, lax.rsqrt(k2), 1.0)
        rq_ref[:, at] = jnp.where(q2 == 1.0, -1.0, rq)
        rk_ref[:, at] = jnp.where(k2 == 1.0, -1.0, rk)
        qs = (q * rq * scale_ref[:, at]).astype(BF16)
        kn = (k * rk).astype(BF16)
        qs_ref[:, at] = qs
        kn_ref[:, at] = kn
        v_ref[:, at] = v
        bias = bias_ref[:, g * per * SPAN : (g + 1) * per * SPAN]
        expo = []
        for w in range(windows):
            rows = slice(w * SPAN, (w + 1) * SPAN)
            kb = jnp.concatenate([kn[rows]] * per, 0) * mask
            expo.append(jnp.exp(dot(qs[rows], kb, NT) + bias))
        expo = jnp.concatenate(expo, 0)
        p = (expo / dot(expo.astype(BF16), key_ones)).astype(BF16)
        p_ref[g * windows * SPAN : (g + 1) * windows * SPAN, :] = p
        for w in range(windows):
            rows = slice(w * SPAN, (w + 1) * SPAN)
            vb = jnp.concatenate([v[rows]] * per, 0) * mask
            mixed_ref[rows, at] = dot(p[rows], vb).astype(BF16)
    u1, i1 = norm_parts(dot(mixed_ref[...], w_proj[...]))
    u1_ref[...] = u1
    i1_ref[...] = i1
    h1 = (x + u1 * gain_attn[...]).astype(BF16)
    mlp = jnp.zeros(x.shape, F32)
    step = width
    for c in range(w_fc1.shape[1] // step):
        cols = slice(c * step, (c + 1) * step)
        z = dot(h1, w_fc1[:, cols])
        zz = z * z
        t = jnp.tanh(GELU_A * z * (1.0 + GELU_B * zz))
        half = 0.5 * (1.0 + t)
        slope = GELU_A + 3.0 * GELU_A * GELU_B * zz
        dg_ref[:, cols] = (half + 0.5 * z * (1.0 - t * t) * slope).astype(BF16)
        mlp = mlp + dot((z * half).astype(BF16), w_fc2[cols, :])
    u2, i2 = norm_parts(mlp)
    u2_ref[...] = u2
    i2_ref[...] = i2
    out_ref[...] = from_windows(h1.astype(F32) + u2 * gain_mlp[...]).astype(BF16)


def unit_back(cot, unit, inv, sum_ones):
    along = split_dot(cot * unit, sum_ones)
    part = jnp.where(inv < 0.0, 0.5, jnp.where(inv < 1.0, 1.0, 0.0))
    return jnp.abs(inv) * (cot - part * unit * along)


def backward_kernel(
    cot_ref, w_qkv, w_proj, w_fc1, w_fc2, gain_attn, gain_mlp, scale_ref,
    qs_ref, kn_ref, v_ref, rq_ref, rk_ref, p_ref, mixed_ref, u1_ref, i1_ref, dg_ref, u2_ref, i2_ref,
    grad_ref, dm_ref,
):
    width = cot_ref.shape[-1]
    per = p_ref.shape[1] // SPAN
    head = LANES // per
    cot = to_windows(cot_ref[...].astype(F32))
    windows = cot.shape[0] // SPAN
    dmlp = norm_back(cot * gain_mlp[...], u2_ref[...], i2_ref[...]).astype(BF16)
    dh = jnp.zeros(cot.shape, F32)
    step = width
    for c in range(w_fc1.shape[1] // step):
        cols = slice(c * step, (c + 1) * step)
        dz = dot(dmlp, w_fc2[cols, :], NT) * dg_ref[:, cols].astype(F32)
        dh = dh + dot(dz.astype(BF16), w_fc1[:, cols], NT)
    dh = (cot + dh).astype(BF16).astype(F32)
    dproj = norm_back(dh * gain_attn[...], u1_ref[...], i1_ref[...]).astype(BF16)
    dm_ref[...] = dot(dproj, w_proj[...], NT).astype(BF16)
    sum_ones = block_ones(LANES, LANES, head, head)
    sum_ones = jnp.concatenate([sum_ones, sum_ones], 0)
    mask = block_ones(per * SPAN, LANES, SPAN, head)
    mask32 = mask.astype(F32)
    dx = dh
    for g in range(width // LANES):
        at = slice(g * LANES, (g + 1) * LANES)
        dm = dm_ref[:, at]
        own = (dm.astype(F32) * mixed_ref[:, at].astype(F32)).astype(BF16)
        both = jnp.concatenate([dm, own], 1)
        qs = qs_ref[:, at]
        kn = kn_ref[:, at]
        v = v_ref[:, at]
        dqs, dks, dvs = [], [], []
        for w in range(windows):
            rows = slice(w * SPAN, (w + 1) * SPAN)
            kb = jnp.concatenate([kn[rows]] * per, 0) * mask
            vb = jnp.concatenate([v[rows]] * per, 0) * mask
            p = p_ref[(g * windows + w) * SPAN : (g * windows + w + 1) * SPAN, :]
            spread = dot(both[rows], jnp.concatenate([vb, -mask], 1), NT)
            ds = (p.astype(F32) * spread).astype(BF16)
            dqs.append(dot(ds, kb))
            dkb = dot(ds, qs[rows], TN) * mask32
            dvb = dot(p, dm[rows], TN) * mask32
            dks.append(sum(dkb[i * SPAN : (i + 1) * SPAN] for i in range(per)))
            dvs.append(sum(dvb[i * SPAN : (i + 1) * SPAN] for i in range(per)))
        scale = scale_ref[:, at]
        dq = unit_back(
            jnp.concatenate(dqs, 0) * scale, qs.astype(F32) / scale, rq_ref[:, at], sum_ones
        )
        dk = unit_back(jnp.concatenate(dks, 0), kn.astype(F32), rk_ref[:, at], sum_ones)
        dv = jnp.concatenate(dvs, 0)
        dx = dx + dot(dq.astype(BF16), w_qkv[:, at], NT)
        dx = dx + dot(dk.astype(BF16), w_qkv[:, width + g * LANES : width + (g + 1) * LANES], NT)
        dx = dx + dot(dv.astype(BF16), w_qkv[:, 2 * width + g * LANES : 2 * width + (g + 1) * LANES], NT)
    grad_ref[...] = from_windows(dx).astype(BF16)


def order_kernel(tok_rows, tok_cols, row_devs, col_devs, feat_ref, patch_ref, cover_ref, w_ref, send_ref, pos_ref):
    slots, width = feat_ref.shape
    devs = row_devs * col_devs
    grid_cols = tok_cols * col_devs
    patch = patch_ref[...]
    row = patch // grid_cols
    col = patch % grid_cols
    target = row // tok_rows * col_devs + col // tok_cols
    hit = lax.broadcasted_iota(jnp.int32, (devs, slots), 0) == target
    i = lax.broadcasted_iota(jnp.int32, (slots, slots), 0)
    j = lax.broadcasted_iota(jnp.int32, (slots, slots), 1)
    earlier = jnp.where(i < j, 1.0, 0.0).astype(BF16)
    count = dot(jnp.where(hit, 1.0, 0.0).astype(BF16), earlier)
    rank = jnp.sum(jnp.where(hit, count, 0.0), 0, keepdims=True).astype(jnp.int32)
    pos = target * (slots // devs) + rank
    pos_ref[...] = pos
    place = jnp.where(i == pos, 1.0, 0.0).astype(BF16)
    query = dot(feat_ref[...], w_ref[...]).astype(BF16)
    send_ref[:, :width] = dot(place, query).astype(BF16)
    which = lax.broadcasted_iota(jnp.int32, (LANES, slots), 0)
    meta = jnp.where(which == 0, (row % tok_rows).astype(F32), 0.0)
    meta = jnp.where(which == 1, (col % tok_cols).astype(F32), meta)
    for c in range(3):
        meta = jnp.where(which == 2 + c, cover_ref[c : c + 1, :].astype(F32), meta)
    send_ref[:, width:] = dot(place, meta.astype(BF16), NT).astype(BF16)


def readout_kernel(cols, piece_ref, ext_ref, w_ref, scale_ref, head, out_ref, table_ref):
    width = out_ref.shape[1]
    rows = out_ref.shape[0]
    cells = ext_ref.shape[0]
    sum_ones = block_ones(LANES, LANES, head, head)
    sum_ones = jnp.concatenate([sum_ones, sum_ones], 0)

    @pl.when(pl.program_id(0) == 0)
    def _():
        for g in range(width // LANES):
            at = slice(g * LANES, (g + 1) * LANES)
            k = dot(ext_ref[...], w_ref[:, at]).astype(BF16).astype(F32)
            k2 = split_dot(k * k, sum_ones)
            table_ref[:, at] = (k * jnp.where(k2 > 1.0, lax.rsqrt(k2), 1.0)).astype(BF16)
        table_ref[:, width:] = dot(ext_ref[...], w_ref[:, width:]).astype(BF16)

    meta = piece_ref[:, width : width + LANES].astype(F32)
    base = (meta[:, 0:1] * cols + meta[:, 1:2]).astype(jnp.int32)
    lane = lax.broadcasted_iota(jnp.int32, (rows, cells), 1)
    picks = jnp.concatenate(
        [jnp.where(lane == base + step, 1.0, 0.0).astype(BF16) for step in (0, 1, cols, cols + 1)], 0
    )
    flags = [jnp.broadcast_to(meta[:, 2 + c : 3 + c], (rows, LANES)) for c in range(3)]
    for g in range(width // LANES):
        at = slice(g * LANES, (g + 1) * LANES)
        q = piece_ref[:, at].astype(F32)
        q2 = split_dot(q * q, sum_ones)
        q = q * jnp.where(q2 > 1.0, lax.rsqrt(q2), 1.0) * scale_ref[:, at]
        both = jnp.concatenate([table_ref[:, at], table_ref[:, width + g * LANES : width + (g + 1) * LANES]], 1)
        got = dot(picks, both)
        scores = split_dot(jnp.concatenate([q] * 4, 0) * got[:, :LANES], sum_ones)
        total, mix = 0.0, 0.0
        for c in range(4):
            at_c = slice(c * rows, (c + 1) * rows)
            expo = jnp.exp(scores[at_c])
            if c > 0:
                expo = expo * flags[c - 1]
            total = total + expo
            mix = mix + expo * got[at_c, LANES:]
        out_ref[:, at] = (mix / total).astype(BF16)


def finish_kernel(ret_ref, pos_ref, feat_ref, w_ref, live_ref, out_ref):
    slots = feat_ref.shape[0]
    i = lax.broadcasted_iota(jnp.int32, (slots, slots), 0)
    place = jnp.where(i == pos_ref[...], 1.0, 0.0).astype(BF16)
    mix = dot(place, ret_ref[...], TN).astype(BF16)
    updated = feat_ref[...].astype(F32) + dot(mix, w_ref[...])
    slot = lax.broadcasted_iota(jnp.int32, updated.shape, 0)
    out_ref[...] = jnp.where(slot < live_ref[0], updated, 0.0).astype(BF16)


def bias_kernel(table_ref, out_ref):
    size, lanes = table_ref.shape
    heads = lanes // WIN
    table = table_ref[...]
    high = table.astype(BF16)
    low = (table - high.astype(F32)).astype(BF16)
    m_b = lax.broadcasted_iota(jnp.int32, (2 * SPAN, size), 0)
    entry = lax.broadcasted_iota(jnp.int32, (2 * SPAN, size), 1)
    start = m_b // WIN * (2 * WIN - 1) + m_b % WIN + WIN - 1
    lane_d = lax.broadcasted_iota(jnp.int32, (size, lanes), 1) // heads
    edge = jnp.zeros((2 * SPAN, 2 * lanes), F32)
    for d in range(WIN):
        pick = jnp.where(entry == start - d, 1.0, 0.0).astype(BF16)
        here = jnp.where(lane_d == d, 1.0, 0.0).astype(BF16)
        edge = edge + dot(pick, jnp.concatenate([high * here, low * here], 1))
    rows = [edge[(WIN - 1 - c) * WIN : (WIN - 1 - c) * WIN + SPAN, :] for c in range(WIN)]
    both = jnp.concatenate(
        [
            jnp.concatenate([row[:, :lanes] for row in rows], 1),
            jnp.concatenate([row[:, lanes:] for row in rows], 1),
        ],
        0,
    ).astype(BF16)
    step = 2 * LANES
    source = lax.broadcasted_iota(jnp.int32, (WIN * lanes, step), 0)
    for part in range(heads * SPAN // step):
        col = lax.broadcasted_iota(jnp.int32, (1, step), 1) + part * step
        want = col // WIN % WIN * lanes + col % WIN * heads + col // SPAN
        got = dot(both, jnp.where(source == want, 1.0, 0.0).astype(BF16))
        out_ref[:, part * step : (part + 1) * step] = got[:SPAN] + got[SPAN:]


def moved(piece, rows, cols):
    n, m = lax.axis_size("gx"), lax.axis_size("gy")
    route = [
        (i * m + j, (i + rows) % n * m + (j + cols) % m) for i in range(n) for j in range(m)
    ]
    return lax.ppermute(piece, ("gx", "gy"), route)


def params(mib=24):
    return pltpu.CompilerParams(vmem_limit_bytes=mib * 1024 * 1024)


def local(
    wave_tokens, grad_out, w_qkv, w_proj, w_fc1, w_fc2, gain_attn, gain_mlp, attn_scale,
    bias_table, r_wq, r_wkv, r_wo, read_scale, floe_feat, floe_count, floe_patch, floe_cover,
):
    tok_rows, tok_cols, width = wave_tokens.shape
    heads = attn_scale.shape[0]
    head = width // heads
    tokens = tok_rows * tok_cols
    hidden = w_fc1.shape[1]
    row_devs, col_devs = lax.axis_size("gx"), lax.axis_size("gy")
    feat = floe_feat[0]
    slots = feat.shape[0]
    vmem = pl.BlockSpec(memory_space=pltpu.VMEM)
    s = SHIFT

    row_in = moved(jnp.concatenate([wave_tokens[:s, s:], grad_out[:s, s:]], 0), -1, 0)
    col_in = moved(jnp.concatenate([wave_tokens[s:, :s], grad_out[s:, :s]], 0), 0, -1)
    cor_in = moved(jnp.concatenate([wave_tokens[:s, :s], grad_out[:s, :s]], 0), -1, -1)

    def ahead(field, part):
        upper = jnp.concatenate([field[s:, s:], col_in[part * (tok_rows - s) : (part + 1) * (tok_rows - s)]], 1)
        lower = jnp.concatenate([row_in[part * s : (part + 1) * s], cor_in[part * s : (part + 1) * s]], 1)
        return jnp.concatenate([upper, lower], 0)

    send, pos = pl.pallas_call(
        lambda *refs: order_kernel(tok_rows, tok_cols, row_devs, col_devs, *refs),
        out_shape=(
            jax.ShapeDtypeStruct((slots, width + LANES), BF16),
            jax.ShapeDtypeStruct((1, slots), jnp.int32),
        ),
        in_specs=[vmem] * 4,
        out_specs=(vmem, vmem),
        compiler_params=params(),
        cost_estimate=pl.CostEstimate(flops=3000000000, bytes_accessed=3000000, transcendentals=0),
    )(feat, floe_patch, floe_cover[0], r_wq)
    piece = lax.all_to_all(send, ("gx", "gy"), split_axis=0, concat_axis=0, tiled=True)

    bias = pl.pallas_call(
        bias_kernel,
        out_shape=jax.ShapeDtypeStruct((SPAN, heads * SPAN), F32),
        in_specs=[vmem],
        out_specs=vmem,
        compiler_params=params(),
        cost_estimate=pl.CostEstimate(flops=1500000000, bytes_accessed=1000000, transcendentals=0),
    )(jnp.tile(jnp.pad(bias_table, ((0, 0), (0, -bias_table.shape[1] % LANES))).T, (1, WIN)))
    scale = jnp.repeat(attn_scale, head)[None]
    gain_a, gain_m = gain_attn[None], gain_mlp[None]
    rolled = ahead(wave_tokens, 0)
    cot = ahead(grad_out, 1)
    wide = jax.ShapeDtypeStruct((tokens, width), BF16)
    wide32 = jax.ShapeDtypeStruct((tokens, width), F32)
    one = jax.ShapeDtypeStruct((tokens, 1), F32)
    res = pl.pallas_call(
        forward_kernel,
        out_shape=(
            jax.ShapeDtypeStruct(wave_tokens.shape, BF16),
            wide, wide, wide, wide32, wide32,
            jax.ShapeDtypeStruct((tokens * width // LANES, LANES // head * SPAN), BF16),
            wide, wide32, one, jax.ShapeDtypeStruct((tokens, hidden), BF16), wide32, one,
        ),
        in_specs=[vmem] * 9,
        out_specs=(vmem,) * 13,
        compiler_params=params(),
        cost_estimate=pl.CostEstimate(flops=8000000000, bytes_accessed=8000000, transcendentals=1000000),
    )(rolled, w_qkv, w_proj, w_fc1, w_fc2, gain_a, gain_m, scale, bias)
    out = res[0]
    near, far = tok_rows - s + 1, tok_cols - s
    row_out = moved(out[s:, : far + 1], 1, 0)
    col_out = moved(out[:near, far:], 0, 1)
    cor_out = moved(out[s:, far:], 1, 1)
    grad = pl.pallas_call(
        backward_kernel,
        out_shape=jax.ShapeDtypeStruct(wave_tokens.shape, BF16),
        in_specs=[vmem] * 20,
        out_specs=vmem,
        scratch_shapes=[pltpu.VMEM((tokens, width), BF16)],
        compiler_params=params(),
        cost_estimate=pl.CostEstimate(flops=10000000000, bytes_accessed=8000000, transcendentals=0),
    )(cot, w_qkv, w_proj, w_fc1, w_fc2, gain_a, gain_m, scale, *res[1:])
    piece, grad = lax.optimization_barrier((piece, grad))
    row_grad = moved(grad[s:, :far], 1, 0)
    col_grad = moved(grad[: tok_rows - s, far:], 0, 1)
    cor_grad = moved(grad[s:, far:], 1, 1)

    ext = jnp.concatenate(
        [
            jnp.concatenate([cor_out, row_out], 1),
            jnp.concatenate([col_out, out[:near, : far + 1]], 1),
        ],
        0,
    )
    patch_out = ext[:tok_rows, :tok_cols]
    ext_cols = tok_cols + 1
    cells = (tok_rows + 1) * ext_cols
    padded = -(-cells // LANES) * LANES
    table = jnp.pad(ext.reshape(cells, width), ((0, padded - cells), (0, 0)))
    parts = 3
    chunk = slots // parts
    mix = pl.pallas_call(
        lambda a, b, c, d, e, f: readout_kernel(ext_cols, a, b, c, d, head, e, f),
        out_shape=jax.ShapeDtypeStruct((slots, width), BF16),
        grid=(parts,),
        in_specs=[
            pl.BlockSpec((chunk, width + LANES), lambda i: (i, 0)),
            vmem, vmem, vmem,
        ],
        out_specs=pl.BlockSpec((chunk, width), lambda i: (i, 0)),
        scratch_shapes=[pltpu.VMEM((padded, 2 * width), BF16)],
        compiler_params=params(),
        cost_estimate=pl.CostEstimate(flops=8000000000, bytes_accessed=3000000, transcendentals=1000000),
    )(piece, table, r_wkv, jnp.repeat(read_scale, head)[None])
    back = lax.all_to_all(mix, ("gx", "gy"), split_axis=0, concat_axis=0, tiled=True)
    floe_out = pl.pallas_call(
        finish_kernel,
        out_shape=jax.ShapeDtypeStruct((slots, width), BF16),
        in_specs=[vmem] * 4 + [pl.BlockSpec(memory_space=pltpu.SMEM)],
        out_specs=vmem,
        compiler_params=params(),
        cost_estimate=pl.CostEstimate(flops=1500000000, bytes_accessed=3000000, transcendentals=0),
    )(back, pos, feat, r_wo, floe_count)
    grad_in = jnp.concatenate(
        [
            jnp.concatenate([cor_grad, row_grad], 1),
            jnp.concatenate([col_grad, grad[: tok_rows - s, :far]], 1),
        ],
        0,
    )
    return (patch_out, grad_in, floe_out[None])


def solution(mesh):
    grid = P("gx", "gy", None)
    owner = ("gx", "gy")
    in_specs = (grid, grid) + (P(),) * 12 + (P(owner, None, None), P(owner), P(owner, None), P(owner, None, None))
    out_specs = (grid, grid, P(owner, None, None))
    return jax.shard_map(local, mesh=mesh, in_specs=in_specs, out_specs=out_specs, check_vma=False)
```

```python
import jax
import jax.numpy as jnp
from jax import lax
from jax.experimental import pallas as pl
from jax.experimental.pallas import tpu as pltpu
from jax.sharding import PartitionSpec as P

WIN = 8
SHIFT = 4
SPAN = WIN * WIN
LANES = 128
F32 = jnp.float32
BF16 = jnp.bfloat16
GELU_A = 0.7978845608028654
GELU_B = 0.044715
NN = (((1,), (0,)), ((), ()))
NT = (((1,), (1,)), ((), ()))
TN = (((0,), (0,)), ((), ()))


def dot(a, b, dims=NN):
    return lax.dot_general(a, b, dims, preferred_element_type=F32)


def split_dot(values, ones):
    high = values.astype(BF16)
    low = (values - high.astype(F32)).astype(BF16)
    return dot(jnp.concatenate([high, low], 1), ones)


def block_ones(rows, cols, row_size, col_size):
    r = lax.broadcasted_iota(jnp.int32, (rows, cols), 0) // row_size
    c = lax.broadcasted_iota(jnp.int32, (rows, cols), 1) // col_size
    return jnp.where(r == c, 1.0, 0.0).astype(BF16)


def to_windows(block):
    rows, cols, width = block.shape
    parts = [block[:, w * WIN : (w + 1) * WIN, :].reshape(SPAN, width) for w in range(cols // WIN)]
    return jnp.concatenate(parts, 0)


def from_windows(flat):
    count = flat.shape[0] // SPAN
    parts = [flat[w * SPAN : (w + 1) * SPAN].reshape(WIN, WIN, flat.shape[1]) for w in range(count)]
    return jnp.concatenate(parts, 1)


def norm_parts(values):
    mean = jnp.mean(values, -1, keepdims=True)
    centred = values - mean
    inv = lax.rsqrt(jnp.mean(centred * centred, -1, keepdims=True) + 1e-05)
    return centred * inv, inv


def norm_back(cot, unit, inv):
    return inv * (
        cot - jnp.mean(cot, -1, keepdims=True) - unit * jnp.mean(cot * unit, -1, keepdims=True)
    )


def forward_kernel(
    x_ref, w_qkv, w_proj, w_fc1, w_fc2, gain_attn, gain_mlp, scale_ref, bias_ref,
    out_ref, *rest,
):
    kept, (proj_buf, fc1_buf, fc2_buf), held, (sems, kept_sems) = rest[:12], rest[12:15], rest[15:27], rest[27:]
    qs_ref, kn_ref, v_ref, rq_ref, rk_ref, p_ref, mixed_ref, u1_ref, i1_ref, dg_ref, u2_ref, i2_ref = held
    stores = [
        pltpu.make_async_copy(src, dst, kept_sems.at[i]) for i, (src, dst) in enumerate(zip(held, kept))
    ]
    loads = [
        pltpu.make_async_copy(src, dst, sems.at[i])
        for i, (src, dst) in enumerate(((w_proj, proj_buf), (w_fc1, fc1_buf), (w_fc2, fc2_buf)))
    ]
    for load in loads:
        load.start()
    width = x_ref.shape[-1]
    head = width // (bias_ref.shape[1] // SPAN)
    per = LANES // head
    x = to_windows(x_ref[...].astype(F32))
    xb = x.astype(BF16)
    windows = x.shape[0] // SPAN
    sum_ones = block_ones(LANES, LANES, head, head)
    sum_ones = jnp.concatenate([sum_ones, sum_ones], 0)
    mask = block_ones(per * SPAN, LANES, SPAN, head)
    key_ones = block_ones(per * SPAN, per * SPAN, SPAN, SPAN)
    for g in range(width // LANES):
        at = slice(g * LANES, (g + 1) * LANES)
        q = dot(xb, w_qkv[:, at]).astype(BF16).astype(F32)
        k = dot(xb, w_qkv[:, width + g * LANES : width + (g + 1) * LANES]).astype(BF16).astype(F32)
        v = dot(xb, w_qkv[:, 2 * width + g * LANES : 2 * width + (g + 1) * LANES]).astype(BF16)
        q2 = split_dot(q * q, sum_ones)
        k2 = split_dot(k * k, sum_ones)
        rq = jnp.where(q2 > 1.0, lax.rsqrt(q2), 1.0)
        rk = jnp.where(k2 > 1.0, lax.rsqrt(k2), 1.0)
        rq_ref[:, at] = jnp.where(q2 == 1.0, -1.0, rq)
        rk_ref[:, at] = jnp.where(k2 == 1.0, -1.0, rk)
        qs = (q * rq * scale_ref[:, at]).astype(BF16)
        kn = (k * rk).astype(BF16)
        qs_ref[:, at] = qs
        kn_ref[:, at] = kn
        v_ref[:, at] = v
        bias = bias_ref[:, g * per * SPAN : (g + 1) * per * SPAN]
        expo = []
        for w in range(windows):
            rows = slice(w * SPAN, (w + 1) * SPAN)
            kb = jnp.concatenate([kn[rows]] * per, 0) * mask
            expo.append(jnp.exp(dot(qs[rows], kb, NT) + bias))
        expo = jnp.concatenate(expo, 0)
        p = (expo / dot(expo.astype(BF16), key_ones)).astype(BF16)
        p_ref[g * windows * SPAN : (g + 1) * windows * SPAN, :] = p
        for w in range(windows):
            rows = slice(w * SPAN, (w + 1) * SPAN)
            vb = jnp.concatenate([v[rows]] * per, 0) * mask
            mixed_ref[rows, at] = dot(p[rows], vb).astype(BF16)
    for store in stores[:7]:
        store.start()
    loads[0].wait()
    u1, i1 = norm_parts(dot(mixed_ref[...], proj_buf[...]))
    u1_ref[...] = u1
    i1_ref[...] = jnp.broadcast_to(i1, i1_ref.shape)
    for store in stores[7:9]:
        store.start()
    h1 = (x + u1 * gain_attn[...]).astype(BF16)
    mlp = jnp.zeros(x.shape, F32)
    step = width
    loads[1].wait()
    loads[2].wait()
    for c in range(w_fc1.shape[1] // step):
        cols = slice(c * step, (c + 1) * step)
        z = dot(h1, fc1_buf[:, cols])
        zz = z * z
        t = jnp.tanh(GELU_A * z * (1.0 + GELU_B * zz))
        half = 0.5 * (1.0 + t)
        slope = GELU_A + 3.0 * GELU_A * GELU_B * zz
        dg_ref[:, cols] = (half + 0.5 * z * (1.0 - t * t) * slope).astype(BF16)
        mlp = mlp + dot((z * half).astype(BF16), fc2_buf[cols, :])
    u2, i2 = norm_parts(mlp)
    u2_ref[...] = u2
    i2_ref[...] = jnp.broadcast_to(i2, i2_ref.shape)
    for store in stores[9:]:
        store.start()
    out_ref[...] = from_windows(h1.astype(F32) + u2 * gain_mlp[...]).astype(BF16)
    for store in stores:
        store.wait()


def unit_back(cot, unit, inv, sum_ones):
    along = split_dot(cot * unit, sum_ones)
    part = jnp.where(inv < 0.0, 0.5, jnp.where(inv < 1.0, 1.0, 0.0))
    return jnp.abs(inv) * (cot - part * unit * along)


def backward_kernel(
    cot_ref, qkv_hbm, proj_hbm, fc1_hbm, fc2_hbm, gain_attn, gain_mlp, scale_ref, *rest
):
    kept, (grad_ref, dm_ref), (w_proj, w_fc1, w_fc2, w_qkv), held, (sems,) = (
        rest[:12], rest[12:14], rest[14:18], rest[18:30], rest[30:]
    )
    qs_ref, kn_ref, v_ref, rq_ref, rk_ref, p_ref, mixed_ref, u1_ref, i1_ref, dg_ref, u2_ref, i2_ref = held
    pairs = list(zip(kept, held)) + [
        (proj_hbm, w_proj), (fc1_hbm, w_fc1), (fc2_hbm, w_fc2), (qkv_hbm, w_qkv)
    ]
    loads = [pltpu.make_async_copy(src, dst, sems.at[i]) for i, (src, dst) in enumerate(pairs)]
    stages = ((10, 11), (14, 9, 13), (7, 8, 12), (0, 1, 2, 3, 4, 5, 6, 15))
    for stage in stages:
        for i in stage:
            loads[i].start()

    def arrive(stage):
        for i in stages[stage]:
            loads[i].wait()

    width = cot_ref.shape[-1]
    per = p_ref.shape[1] // SPAN
    head = LANES // per
    cot = to_windows(cot_ref[...].astype(F32))
    windows = cot.shape[0] // SPAN
    arrive(0)
    dmlp = norm_back(cot * gain_mlp[...], u2_ref[...], i2_ref[:, :1]).astype(BF16)
    arrive(1)
    dh = jnp.zeros(cot.shape, F32)
    step = width
    for c in range(w_fc1.shape[1] // step):
        cols = slice(c * step, (c + 1) * step)
        dz = dot(dmlp, w_fc2[cols, :], NT) * dg_ref[:, cols].astype(F32)
        dh = dh + dot(dz.astype(BF16), w_fc1[:, cols], NT)
    dh = (cot + dh).astype(BF16).astype(F32)
    arrive(2)
    dproj = norm_back(dh * gain_attn[...], u1_ref[...], i1_ref[:, :1]).astype(BF16)
    dm_ref[...] = dot(dproj, w_proj[...], NT).astype(BF16)
    sum_ones = block_ones(LANES, LANES, head, head)
    sum_ones = jnp.concatenate([sum_ones, sum_ones], 0)
    mask = block_ones(per * SPAN, LANES, SPAN, head)
    mask32 = mask.astype(F32)
    dx = dh
    arrive(3)
    for g in range(width // LANES):
        at = slice(g * LANES, (g + 1) * LANES)
        dm = dm_ref[:, at]
        own = (dm.astype(F32) * mixed_ref[:, at].astype(F32)).astype(BF16)
        both = jnp.concatenate([dm, own], 1)
        qs = qs_ref[:, at]
        kn = kn_ref[:, at]
        v = v_ref[:, at]
        dqs, dks, dvs = [], [], []
        for w in range(windows):
            rows = slice(w * SPAN, (w + 1) * SPAN)
            kb = jnp.concatenate([kn[rows]] * per, 0) * mask
            vb = jnp.concatenate([v[rows]] * per, 0) * mask
            p = p_ref[(g * windows + w) * SPAN : (g * windows + w + 1) * SPAN, :]
            spread = dot(both[rows], jnp.concatenate([vb, -mask], 1), NT)
            ds = (p.astype(F32) * spread).astype(BF16)
            dqs.append(dot(ds, kb))
            dkb = dot(ds, qs[rows], TN) * mask32
            dvb = dot(p, dm[rows], TN) * mask32
            dks.append(sum(dkb[i * SPAN : (i + 1) * SPAN] for i in range(per)))
            dvs.append(sum(dvb[i * SPAN : (i + 1) * SPAN] for i in range(per)))
        scale = scale_ref[:, at]
        dq = unit_back(
            jnp.concatenate(dqs, 0) * scale, qs.astype(F32) / scale, rq_ref[:, at], sum_ones
        )
        dk = unit_back(jnp.concatenate(dks, 0), kn.astype(F32), rk_ref[:, at], sum_ones)
        dv = jnp.concatenate(dvs, 0)
        dx = dx + dot(dq.astype(BF16), w_qkv[:, at], NT)
        dx = dx + dot(dk.astype(BF16), w_qkv[:, width + g * LANES : width + (g + 1) * LANES], NT)
        dx = dx + dot(dv.astype(BF16), w_qkv[:, 2 * width + g * LANES : 2 * width + (g + 1) * LANES], NT)
    grad_ref[...] = from_windows(dx).astype(BF16)


def order_kernel(tok_rows, tok_cols, row_devs, col_devs, feat_ref, patch_ref, cover_ref, w_ref, send_ref, pos_ref, feat_buf, w_buf, sems):
    slots, width = feat_ref.shape
    loads = [
        pltpu.make_async_copy(feat_ref, feat_buf, sems.at[0]),
        pltpu.make_async_copy(w_ref, w_buf, sems.at[1]),
    ]
    for load in loads:
        load.start()
    devs = row_devs * col_devs
    grid_cols = tok_cols * col_devs
    patch = patch_ref[...]
    row = patch // grid_cols
    col = patch % grid_cols
    target = row // tok_rows * col_devs + col // tok_cols
    hit = lax.broadcasted_iota(jnp.int32, (devs, slots), 0) == target
    i = lax.broadcasted_iota(jnp.int32, (slots, slots), 0)
    j = lax.broadcasted_iota(jnp.int32, (slots, slots), 1)
    earlier = jnp.where(i < j, 1.0, 0.0).astype(BF16)
    count = dot(jnp.where(hit, 1.0, 0.0).astype(BF16), earlier)
    rank = jnp.sum(jnp.where(hit, count, 0.0), 0, keepdims=True).astype(jnp.int32)
    pos = target * (slots // devs) + rank
    pos_ref[...] = pos
    place = jnp.where(i == pos, 1.0, 0.0).astype(BF16)
    for load in loads:
        load.wait()
    query = dot(feat_buf[...], w_buf[...]).astype(BF16)
    send_ref[:, :width] = dot(place, query).astype(BF16)
    which = lax.broadcasted_iota(jnp.int32, (LANES, slots), 0)
    meta = jnp.where(which == 0, (row % tok_rows).astype(F32), 0.0)
    meta = jnp.where(which == 1, (col % tok_cols).astype(F32), meta)
    for c in range(3):
        meta = jnp.where(which == 2 + c, cover_ref[c : c + 1, :].astype(F32), meta)
    send_ref[:, width:] = dot(place, meta.astype(BF16), NT).astype(BF16)


def readout_kernel(cols, piece_ref, ext_ref, w_ref, scale_ref, head, out_ref, table_ref):
    width = out_ref.shape[1]
    rows = out_ref.shape[0]
    cells = ext_ref.shape[0]
    sum_ones = block_ones(LANES, LANES, head, head)
    sum_ones = jnp.concatenate([sum_ones, sum_ones], 0)

    @pl.when(pl.program_id(0) == 0)
    def _():
        for g in range(width // LANES):
            at = slice(g * LANES, (g + 1) * LANES)
            k = dot(ext_ref[...], w_ref[:, at]).astype(BF16).astype(F32)
            k2 = split_dot(k * k, sum_ones)
            table_ref[:, at] = (k * jnp.where(k2 > 1.0, lax.rsqrt(k2), 1.0)).astype(BF16)
        table_ref[:, width:] = dot(ext_ref[...], w_ref[:, width:]).astype(BF16)

    meta = piece_ref[:, width : width + LANES].astype(F32)
    base = (meta[:, 0:1] * cols + meta[:, 1:2]).astype(jnp.int32)
    lane = lax.broadcasted_iota(jnp.int32, (rows, cells), 1)
    picks = jnp.concatenate(
        [jnp.where(lane == base + step, 1.0, 0.0).astype(BF16) for step in (0, 1, cols, cols + 1)], 0
    )
    flags = [jnp.broadcast_to(meta[:, 2 + c : 3 + c], (rows, LANES)) for c in range(3)]
    for g in range(width // LANES):
        at = slice(g * LANES, (g + 1) * LANES)
        q = piece_ref[:, at].astype(F32)
        q2 = split_dot(q * q, sum_ones)
        q = q * jnp.where(q2 > 1.0, lax.rsqrt(q2), 1.0) * scale_ref[:, at]
        both = jnp.concatenate([table_ref[:, at], table_ref[:, width + g * LANES : width + (g + 1) * LANES]], 1)
        got = dot(picks, both)
        scores = split_dot(jnp.concatenate([q] * 4, 0) * got[:, :LANES], sum_ones)
        total, mix = 0.0, 0.0
        for c in range(4):
            at_c = slice(c * rows, (c + 1) * rows)
            expo = jnp.exp(scores[at_c])
            if c > 0:
                expo = expo * flags[c - 1]
            total = total + expo
            mix = mix + expo * got[at_c, LANES:]
        out_ref[:, at] = (mix / total).astype(BF16)


def finish_kernel(ret_ref, pos_ref, feat_ref, w_ref, live_ref, out_ref):
    slots = feat_ref.shape[0]
    i = lax.broadcasted_iota(jnp.int32, (slots, slots), 0)
    place = jnp.where(i == pos_ref[...], 1.0, 0.0).astype(BF16)
    mix = dot(place, ret_ref[...], TN).astype(BF16)
    updated = feat_ref[...].astype(F32) + dot(mix, w_ref[...])
    slot = lax.broadcasted_iota(jnp.int32, updated.shape, 0)
    out_ref[...] = jnp.where(slot < live_ref[0], updated, 0.0).astype(BF16)


def bias_kernel(table_ref, out_ref):
    size, lanes = table_ref.shape
    heads = lanes // WIN
    table = table_ref[...]
    high = table.astype(BF16)
    low = (table - high.astype(F32)).astype(BF16)
    m_b = lax.broadcasted_iota(jnp.int32, (2 * SPAN, size), 0)
    entry = lax.broadcasted_iota(jnp.int32, (2 * SPAN, size), 1)
    start = m_b // WIN * (2 * WIN - 1) + m_b % WIN + WIN - 1
    lane_d = lax.broadcasted_iota(jnp.int32, (size, lanes), 1) // heads
    edge = jnp.zeros((2 * SPAN, 2 * lanes), F32)
    for d in range(WIN):
        pick = jnp.where(entry == start - d, 1.0, 0.0).astype(BF16)
        here = jnp.where(lane_d == d, 1.0, 0.0).astype(BF16)
        edge = edge + dot(pick, jnp.concatenate([high * here, low * here], 1))
    rows = [edge[(WIN - 1 - c) * WIN : (WIN - 1 - c) * WIN + SPAN, :] for c in range(WIN)]
    both = jnp.concatenate(
        [
            jnp.concatenate([row[:, :lanes] for row in rows], 1),
            jnp.concatenate([row[:, lanes:] for row in rows], 1),
        ],
        0,
    ).astype(BF16)
    step = 2 * LANES
    source = lax.broadcasted_iota(jnp.int32, (WIN * lanes, step), 0)
    for part in range(heads * SPAN // step):
        col = lax.broadcasted_iota(jnp.int32, (1, step), 1) + part * step
        want = col // WIN % WIN * lanes + col % WIN * heads + col // SPAN
        got = dot(both, jnp.where(source == want, 1.0, 0.0).astype(BF16))
        out_ref[:, part * step : (part + 1) * step] = got[:SPAN] + got[SPAN:]


def moved(piece, rows, cols):
    n, m = lax.axis_size("gx"), lax.axis_size("gy")
    route = [
        (i * m + j, (i + rows) % n * m + (j + cols) % m) for i in range(n) for j in range(m)
    ]
    return lax.ppermute(piece, ("gx", "gy"), route)


def params(mib=24):
    return pltpu.CompilerParams(vmem_limit_bytes=mib * 1024 * 1024)


def local(
    wave_tokens, grad_out, w_qkv, w_proj, w_fc1, w_fc2, gain_attn, gain_mlp, attn_scale,
    bias_table, r_wq, r_wkv, r_wo, read_scale, floe_feat, floe_count, floe_patch, floe_cover,
):
    tok_rows, tok_cols, width = wave_tokens.shape
    heads = attn_scale.shape[0]
    head = width // heads
    tokens = tok_rows * tok_cols
    hidden = w_fc1.shape[1]
    row_devs, col_devs = lax.axis_size("gx"), lax.axis_size("gy")
    feat = floe_feat[0]
    slots = feat.shape[0]
    vmem = pl.BlockSpec(memory_space=pltpu.VMEM)
    anywhere = pl.BlockSpec(memory_space=pltpu.HBM)
    s = SHIFT

    row_in = moved(jnp.concatenate([wave_tokens[:s, s:], grad_out[:s, s:]], 0), -1, 0)
    col_in = moved(jnp.concatenate([wave_tokens[s:, :s], grad_out[s:, :s]], 0), 0, -1)
    cor_in = moved(jnp.concatenate([wave_tokens[:s, :s], grad_out[:s, :s]], 0), -1, -1)

    def ahead(field, part):
        upper = jnp.concatenate([field[s:, s:], col_in[part * (tok_rows - s) : (part + 1) * (tok_rows - s)]], 1)
        lower = jnp.concatenate([row_in[part * s : (part + 1) * s], cor_in[part * s : (part + 1) * s]], 1)
        return jnp.concatenate([upper, lower], 0)

    send, pos = pl.pallas_call(
        lambda *refs: order_kernel(tok_rows, tok_cols, row_devs, col_devs, *refs),
        out_shape=(
            jax.ShapeDtypeStruct((slots, width + LANES), BF16),
            jax.ShapeDtypeStruct((1, slots), jnp.int32),
        ),
        in_specs=[anywhere, vmem, vmem, anywhere],
        out_specs=(vmem, vmem),
        scratch_shapes=[
            pltpu.VMEM(feat.shape, BF16),
            pltpu.VMEM(r_wq.shape, BF16),
            pltpu.SemaphoreType.DMA((2,)),
        ],
        compiler_params=params(58),
        cost_estimate=pl.CostEstimate(flops=3000000000, bytes_accessed=3000000, transcendentals=0),
    )(feat, floe_patch, floe_cover[0], r_wq)
    piece = lax.all_to_all(send, ("gx", "gy"), split_axis=0, concat_axis=0, tiled=True)

    bias = pl.pallas_call(
        bias_kernel,
        out_shape=jax.ShapeDtypeStruct((SPAN, heads * SPAN), F32),
        in_specs=[vmem],
        out_specs=vmem,
        compiler_params=params(),
        cost_estimate=pl.CostEstimate(flops=1500000000, bytes_accessed=1000000, transcendentals=0),
    )(jnp.tile(jnp.pad(bias_table, ((0, 0), (0, -bias_table.shape[1] % LANES))).T, (1, WIN)))
    scale = jnp.repeat(attn_scale, head)[None]
    gain_a, gain_m = gain_attn[None], gain_mlp[None]
    rolled = ahead(wave_tokens, 0)
    cot = ahead(grad_out, 1)
    wide = jax.ShapeDtypeStruct((tokens, width), BF16)
    wide32 = jax.ShapeDtypeStruct((tokens, width), F32)
    one = jax.ShapeDtypeStruct((tokens, LANES), F32)
    kept = (
        wide, wide, wide, wide32, wide32,
        jax.ShapeDtypeStruct((tokens * width // LANES, LANES // head * SPAN), BF16),
        wide, wide32, one, jax.ShapeDtypeStruct((tokens, hidden), BF16), wide32, one,
    )
    held = [pltpu.VMEM(k.shape, k.dtype) for k in kept]
    weights = [pltpu.VMEM(w.shape, BF16) for w in (w_proj, w_fc1, w_fc2)]
    res = pl.pallas_call(
        forward_kernel,
        out_shape=(jax.ShapeDtypeStruct(wave_tokens.shape, BF16),) + kept,
        in_specs=[vmem, vmem, anywhere, anywhere, anywhere] + [vmem] * 4,
        out_specs=(vmem,) + (anywhere,) * 12,
        scratch_shapes=weights + held + [pltpu.SemaphoreType.DMA((3,)), pltpu.SemaphoreType.DMA((12,))],
        compiler_params=params(58),
        cost_estimate=pl.CostEstimate(flops=8000000000, bytes_accessed=8000000, transcendentals=1000000),
    )(rolled, w_qkv, w_proj, w_fc1, w_fc2, gain_a, gain_m, scale, bias)
    out = res[0]
    near, far = tok_rows - s + 1, tok_cols - s
    row_out = moved(out[s:, : far + 1], 1, 0)
    col_out = moved(out[:near, far:], 0, 1)
    cor_out = moved(out[s:, far:], 1, 1)
    ext = jnp.concatenate(
        [
            jnp.concatenate([cor_out, row_out], 1),
            jnp.concatenate([col_out, out[:near, : far + 1]], 1),
        ],
        0,
    )
    patch_out = ext[:tok_rows, :tok_cols]
    ext_cols = tok_cols + 1
    cells = (tok_rows + 1) * ext_cols
    padded = -(-cells // LANES) * LANES
    table = jnp.pad(ext.reshape(cells, width), ((0, padded - cells), (0, 0)))
    parts = 3
    chunk = slots // parts
    mix = pl.pallas_call(
        lambda a, b, c, d, e, f: readout_kernel(ext_cols, a, b, c, d, head, e, f),
        out_shape=jax.ShapeDtypeStruct((slots, width), BF16),
        grid=(parts,),
        in_specs=[
            pl.BlockSpec((chunk, width + LANES), lambda i: (i, 0)),
            vmem, vmem, vmem,
        ],
        out_specs=pl.BlockSpec((chunk, width), lambda i: (i, 0)),
        scratch_shapes=[pltpu.VMEM((padded, 2 * width), BF16)],
        compiler_params=params(),
        cost_estimate=pl.CostEstimate(flops=8000000000, bytes_accessed=3000000, transcendentals=1000000),
    )(piece, table, r_wkv, jnp.repeat(read_scale, head)[None])
    mix, cot = lax.optimization_barrier((mix, cot))
    back = lax.all_to_all(mix, ("gx", "gy"), split_axis=0, concat_axis=0, tiled=True)
    grad = pl.pallas_call(
        backward_kernel,
        out_shape=jax.ShapeDtypeStruct(wave_tokens.shape, BF16),
        in_specs=[vmem] + [anywhere] * 4 + [vmem] * 3 + [anywhere] * 12,
        out_specs=vmem,
        scratch_shapes=[pltpu.VMEM((tokens, width), BF16)]
        + weights
        + [pltpu.VMEM(w_qkv.shape, BF16)]
        + held
        + [pltpu.SemaphoreType.DMA((16,))],
        compiler_params=params(58),
        cost_estimate=pl.CostEstimate(flops=10000000000, bytes_accessed=8000000, transcendentals=0),
    )(cot, w_qkv, w_proj, w_fc1, w_fc2, gain_a, gain_m, scale, *res[1:])
    row_grad = moved(grad[s:, :far], 1, 0)
    col_grad = moved(grad[: tok_rows - s, far:], 0, 1)
    cor_grad = moved(grad[s:, far:], 1, 1)

    floe_out = pl.pallas_call(
        finish_kernel,
        out_shape=jax.ShapeDtypeStruct((slots, width), BF16),
        in_specs=[vmem] * 4 + [pl.BlockSpec(memory_space=pltpu.SMEM)],
        out_specs=vmem,
        compiler_params=params(),
        cost_estimate=pl.CostEstimate(flops=1500000000, bytes_accessed=3000000, transcendentals=0),
    )(back, pos, feat, r_wo, floe_count)
    grad_in = jnp.concatenate(
        [
            jnp.concatenate([cor_grad, row_grad], 1),
            jnp.concatenate([col_grad, grad[: tok_rows - s, :far]], 1),
        ],
        0,
    )
    return (patch_out, grad_in, floe_out[None])


def solution(mesh):
    grid = P("gx", "gy", None)
    owner = ("gx", "gy")
    in_specs = (grid, grid) + (P(),) * 12 + (P(owner, None, None), P(owner), P(owner, None), P(owner, None, None))
    out_specs = (grid, grid, P(owner, None, None))
    return jax.shard_map(local, mesh=mesh, in_specs=in_specs, out_specs=out_specs, check_vma=False)
```
